32 devices in a mesh: wa: 8 (over z, core), an: 4 (over y, x).
Axes of the slice: x: 2, y: 2, z: 4, core: 2. Of those that a mesh axis runs over, the one named last changes fastest.
Arguments:
- mass_field: float32 [64, 128, 64, 256], P(None, 'wa', 'an'), may hold values from -8 to 8
- factor_one: float32 [256, 64], replicated, may hold values from -0.375 to 0.375
- factor_two: float32 [128, 64], P('wa'), may hold values from -0.5 to 0.5
- factor_four: float32 [64, 16], replicated, may hold values from -0.75 to 0.75
Outputs:
- gram: float32 [64, 64], P('an')
The draws below stay inside these ranges and needn't reach their ends.
All inputs are finite; a program needn't handle non-finite values.
Results may differ from the reference program's by a relative error of at most 0.0001.
Values sent between devices are 32-bit elements; how exact they have to be, the bound alone decides.
A program may use at most 128 MiB of HBM per device.

```python
import jax
import jax.numpy as jnp
from jax import lax

N4 = 64
R1 = 64
R2 = 64
R4 = 16
N1 = 256
C2 = 16
N2 = 128
N3 = 64


def draw_mass_field(key, part):
    key_noise, key_shared, key_profile = jax.random.split(key, 3)
    shared = jax.random.normal(key_shared, (N4, N2, 1, N1), jnp.float32)
    profile = jax.random.uniform(key_profile, (1, 1, N3, 1), jnp.float32, 0.5, 1.5)
    noise = jax.random.normal(key_noise, (N4, N2, N3, N1), jnp.float32)
    values = noise + shared * profile
    return jnp.clip(values, -8.0, 8.0).astype(jnp.float32)


def level_of(own_key, extent, pieces, smallest, largest):
    gain, own = 1.0, jax.random.fold_in(own_key, 6)
    for dim, parts in pieces:
        draws = jnp.exp(jax.random.uniform(jax.random.fold_in(own, dim), (parts,), jnp.float32, smallest / len(pieces), largest / len(pieces)))
        gain = gain * jnp.repeat(draws, extent[dim] // parts).reshape([-1 if axis == dim else 1 for axis in range(len(extent))])
    return gain


def centred(stream_key, dims, deviation, most, shards=(), dtype=jnp.bfloat16):
    drawn = jax.random.normal(stream_key, dims, jnp.float32) * deviation
    if len(shards) > 0:
        drawn = level_of(stream_key, dims, shards, -0.22, 0.18) * drawn
    return jnp.clip(drawn, min=-most, max=most).astype(dtype)


def setup_inputs(seed: int = 0) -> dict:
    seeds = jax.random.split(jax.random.key(seed), 5)
    mass_field = draw_mass_field(jax.random.fold_in(seeds[4], 71), 0)
    factor_one = centred(seeds[1], (N1, R1), N1 ** -0.5, 0.375, (), jnp.float32)
    factor_two = centred(seeds[2], (N2, R2), N2 ** -0.5, 0.5, ((0, 8),), jnp.float32)
    factor_four = centred(seeds[3], (N4, R4), N4 ** -0.5, 0.75, (), jnp.float32)
    return {"mass_field": mass_field, "factor_one": factor_one, "factor_two": factor_two, "factor_four": factor_four}


def reference(mass_field, factor_one, factor_two, factor_four):
    blocks = N2 // C2
    highest = lax.Precision.HIGHEST

    def add_block(index_block, projected):
        begin = (index_block * C2).astype(jnp.int32)
        piece = lax.dynamic_slice_in_dim(mass_field, begin, C2, 1)
        factor_piece = lax.dynamic_slice_in_dim(factor_two, begin, C2, 0)
        reduced = jnp.dot(factor_four.T, piece.reshape(N4, C2 * N3 * N1), precision=highest)
        mixed_rows = jnp.dot(reduced.reshape(R4 * C2 * N3, N1), factor_one, precision=highest)
        mixed_rows = mixed_rows.reshape(R4, C2, N3, R1)
        contribution = jnp.einsum("qjkr,jp->rkqp", mixed_rows, factor_piece, precision=highest)
        return projected + contribution.reshape(R1, N3, R4 * R2)

    start_value = jnp.zeros((R1, N3, R4 * R2), jnp.float32)
    projected = lax.fori_loop(0, blocks, add_block, start_value)
    summed = jnp.einsum("rim,rjm->ij", projected, projected, precision=highest)
    return summed / (R1 * R2 * R4)
```

```python
import functools

import jax
import jax.numpy as jnp
from jax import lax
from jax.experimental import pallas as pl
from jax.experimental.pallas import tpu as pltpu
from jax.sharding import PartitionSpec as P

MESH = pl.DeviceIdType.MESH
F32 = jnp.float32
BF16 = jnp.bfloat16
LANES = 128
SUB = 8


def iota(shape, dim):
    return lax.broadcasted_iota(jnp.int32, shape, dim)


def split(x):
    hi = x.astype(BF16)
    return hi, (x - hi.astype(F32)).astype(BF16)


def dot(a, b):
    return jnp.dot(a, b, preferred_element_type=F32)


def dot_nt(a, b):
    return lax.dot_general(a, b, (((1,), (1,)), ((), ())), preferred_element_type=F32)


def one_hot(shape, row, column):
    return jnp.where(row(iota(shape, 0)) == column(iota(shape, 1)), 1.0, 0.0).astype(BF16)


def near_first(count):
    half = count // 2
    return sorted(range(1, count), key=lambda o: (abs(o - half), o))


def kernel(
    nw, na, chunks, group,
    x_hbm, f1t_ref, f2_ref, f4t_ref, out_ref,
    xbuf, a1, f1s, red, f2all, a2, mix, got, proj, rows, part, part_in, term, term_in,
    x_sem, f2_send, f2_recv, mix_send, mix_recv, row_send, row_recv, part_send, part_recv, term_send, term_recv,
):
    me = lax.axis_index("wa")
    mine = lax.axis_index("an")
    species, fibre, slab, first = x_hbm.shape
    rank_one = f1t_ref.shape[0]
    rank_two = f2_ref.shape[1]
    rank_four = f4t_ref.shape[0]
    width = mix.shape[-1]
    q_groups = rank_four * slab // width
    per = fibre // chunks
    all_fibre = nw * fibre
    kept = rank_two * SUB
    share = kept // na
    wa_offsets = near_first(nw)
    an_offsets = near_first(na)

    def wa_peer(o):
        return lax.rem(me + o, nw)

    def an_peer(o):
        return lax.rem(mine + o, na)

    def load(j):
        return pltpu.make_async_copy(x_hbm.at[:, j], xbuf.at[j], x_sem.at[j])

    def start_load(j, carry):
        load(j).start()
        return carry

    lax.fori_loop(0, fibre, start_load, 0)

    barrier = pltpu.get_barrier_semaphore()
    for o in wa_offsets:
        pl.semaphore_signal(barrier, inc=1, device_id=(wa_peer(o), mine), device_id_type=MESH)
    for o in an_offsets:
        pl.semaphore_signal(barrier, inc=1, device_id=(me, an_peer(o)), device_id_type=MESH)

    f4hi, f4lo = split(f4t_ref[...])
    n1 = rank_four * SUB
    spread = one_hot((n1, rank_four), lambda r: r >> 3, lambda c: c)
    widen = one_hot((species, species * SUB), lambda r: r, lambda c: c >> 3)
    same = (iota((n1, species * SUB), 0) & 7) == (iota((n1, species * SUB), 1) & 7)
    for half, part4 in enumerate((f4hi, f4lo)):
        full = dot(dot(spread, part4).astype(BF16), widen)
        a1[half * n1 : (half + 1) * n1, :] = jnp.where(same, full, 0.0).astype(BF16)
    f1hi, f1lo = split(f1t_ref[...])
    f1s[:rank_one, :] = f1hi
    f1s[rank_one:, :] = f1lo
    f2all[me] = f2_ref[...]

    pl.semaphore_wait(barrier, nw + na - 2)

    def f2_copy(o):
        return pltpu.make_async_remote_copy(
            src_ref=f2all.at[me], dst_ref=f2all.at[me],
            send_sem=f2_send.at[o], recv_sem=f2_recv.at[o],
            device_id=(wa_peer(o), mine), device_id_type=MESH,
        )

    for o in wa_offsets:
        f2_copy(o).start()

    def mix_copy(c, o):
        peer = wa_peer(o)
        return pltpu.make_async_remote_copy(
            src_ref=mix.at[c, peer], dst_ref=got.at[c, me],
            send_sem=mix_send.at[c, o], recv_sem=mix_recv.at[c, o],
            device_id=(peer, mine), device_id_type=MESH,
        )

    def one_fibre(j, c, jj):
        for kh in range(slab // SUB):
            block = xbuf[j, :, kh * SUB : (kh + 1) * SUB, :].reshape(species * SUB, first)
            hi, lo = split(block)
            both = dot(a1[...], hi)
            reduced = both[:n1] + both[n1:] + dot(a1[:n1, :], lo)
            red[jj, :, kh * SUB : (kh + 1) * SUB, :] = reduced.reshape(rank_four, SUB, first)
        hi, lo = split(red[jj].reshape(rank_four * slab, first))
        both = dot_nt(f1s[...], hi)
        mixed = both[:rank_one] + both[rank_one:] + dot_nt(f1s[:rank_one, :], lo)
        for d in range(nw):
            rg, qg = d // q_groups, d % q_groups
            mix[c, d, jj] = mixed[rg * SUB : (rg + 1) * SUB, qg * width : (qg + 1) * width]

    def produce(c, carry):
        for jj in range(per):
            load(c * per + jj).wait()
            one_fibre(c * per + jj, c, jj)
        for o in wa_offsets:
            mix_copy(c, o).start()
        got[c, me] = mix[c, me]
        return carry

    lax.fori_loop(0, chunks, produce, 0)

    for o in wa_offsets:
        f2_copy(o).wait()
    f2hi, f2lo = split(f2all[...].reshape(all_fibre, rank_two))
    spread2 = one_hot((kept, rank_two), lambda r: r >> 3, lambda c: c)
    depth = nw * per * SUB
    same2 = (iota((kept, depth), 0) & 7) == (iota((kept, depth), 1) & 7)
    rows_hi = dot_nt(spread2, f2hi).astype(BF16)
    rows_lo = dot_nt(spread2, f2lo).astype(BF16)

    def expand(c, carry):
        def fibre_of(col):
            unit = col >> 3
            return (unit // per) * fibre + c * per + unit % per

        pick = one_hot((all_fibre, depth), lambda r: r, fibre_of)
        a2[c, :kept, :] = jnp.where(same2, dot(rows_hi, pick), 0.0).astype(BF16)
        a2[c, kept:, :] = jnp.where(same2, dot(rows_lo, pick), 0.0).astype(BF16)
        return carry

    lax.fori_loop(0, chunks, expand, 0)
    proj[...] = jnp.zeros_like(proj)

    def project(c, carry):
        for o in wa_offsets:
            mix_copy(c, o).wait()
        hi, lo = split(got[c].reshape(depth, width))
        both = dot(a2[c], hi)
        proj[...] += both[:kept] + both[kept:] + dot(a2[c, :kept, :], lo)
        return carry

    lax.fori_loop(0, chunks, project, 0)

    def row_copy(o):
        peer = an_peer(o)
        return pltpu.make_async_remote_copy(
            src_ref=proj.at[pl.ds(pl.multiple_of(peer * share, SUB), share)], dst_ref=rows.at[mine],
            send_sem=row_send.at[o], recv_sem=row_recv.at[o],
            device_id=(me, peer), device_id_type=MESH,
        )

    for o in an_offsets:
        row_copy(o).start()
    rows[mine] = proj[pl.ds(pl.multiple_of(mine * share, SUB), share), :]
    for o in an_offsets:
        row_copy(o).wait()

    halves = width // LANES
    stack = jnp.concatenate(
        [
            jnp.concatenate([rows[a, :, h * LANES : (h + 1) * LANES] for a in range(na)], axis=1)
            for h in range(halves)
        ],
        axis=0,
    )
    hi, lo = split(stack)
    thi, tlo = split(stack.T)
    q_row = iota((LANES, LANES), 0) // slab
    q_col = iota((LANES, LANES), 1) // slab
    lane_block = iota((na * slab, LANES), 1) // slab
    total = jnp.zeros((na * slab, LANES), F32)
    for b in range(na):
        at = slice(b * LANES, (b + 1) * LANES)
        wide = dot(thi, hi[:, at]) + dot(thi, lo[:, at]) + dot(tlo, hi[:, at])
        wide = wide.reshape(na, LANES, LANES)
        wide = jnp.where((q_row == q_col)[None], wide, 0.0)
        wide = wide.reshape(na, LANES // slab, slab, LANES).sum(axis=1).reshape(na * slab, LANES)
        shift = LANES // 2
        while shift >= slab:
            wide = wide + pltpu.roll(wide, shift, 1)
            shift //= 2
        total = jnp.where(lane_block == b, wide, total)
    part[...] = total.reshape(na, slab, LANES)

    def part_copy(o):
        peer = an_peer(o)
        return pltpu.make_async_remote_copy(
            src_ref=part.at[peer], dst_ref=part_in.at[mine],
            send_sem=part_send.at[o], recv_sem=part_recv.at[o],
            device_id=(me, peer), device_id_type=MESH,
        )

    for o in an_offsets:
        part_copy(o).start()
    part_in[mine] = part[mine]
    for o in an_offsets:
        part_copy(o).wait()
    term[...] = part_in[...].sum(axis=0)

    def term_copy(o):
        return pltpu.make_async_remote_copy(
            src_ref=term, dst_ref=term_in.at[me],
            send_sem=term_send.at[o], recv_sem=term_recv.at[o],
            device_id=(wa_peer(o), mine), device_id_type=MESH,
        )

    for o in wa_offsets:
        term_copy(o).start()
    term_in[me] = term[...]
    for o in wa_offsets:
        term_copy(o).wait()
    out_ref[...] = term_in[...].sum(axis=0)


def on_device(mass_field, factor_one, factor_two, factor_four):
    nw, na = lax.axis_size("wa"), lax.axis_size("an")
    species, fibre, slab, first = mass_field.shape
    rank_one, rank_two, rank_four = factor_one.shape[1], factor_two.shape[1], factor_four.shape[1]
    chunks = 4
    per = fibre // chunks
    width = rank_one * rank_four * slab // (nw * SUB)
    kept = rank_two * SUB
    share = kept // na
    depth = nw * per * SUB
    dma = pltpu.SemaphoreType.DMA
    vmem = pl.BlockSpec(memory_space=pltpu.VMEM)
    summed = pl.pallas_call(
        functools.partial(kernel, nw, na, chunks, SUB),
        out_shape=jax.ShapeDtypeStruct((slab, LANES), F32),
        in_specs=[pl.BlockSpec(memory_space=pl.ANY), vmem, vmem, vmem],
        out_specs=vmem,
        scratch_shapes=[
            pltpu.VMEM((fibre, species, slab, first), F32),
            pltpu.VMEM((2 * rank_four * SUB, species * SUB), BF16),
            pltpu.VMEM((2 * rank_one, first), BF16),
            pltpu.VMEM((per, rank_four, slab, first), F32),
            pltpu.VMEM((nw, fibre, rank_two), F32),
            pltpu.VMEM((chunks, 2 * kept, depth), BF16),
            pltpu.VMEM((chunks, nw, per, SUB, width), F32),
            pltpu.VMEM((chunks, nw, per, SUB, width), F32),
            pltpu.VMEM((kept, width), F32),
            pltpu.VMEM((na, share, width), F32),
            pltpu.VMEM((na, slab, LANES), F32),
            pltpu.VMEM((na, slab, LANES), F32),
            pltpu.VMEM((slab, LANES), F32),
            pltpu.VMEM((nw, slab, LANES), F32),
            dma((fibre,)),
            dma((nw,)), dma((nw,)),
            dma((chunks, nw)), dma((chunks, nw)),
            dma((na,)), dma((na,)),
            dma((na,)), dma((na,)),
            dma((nw,)), dma((nw,)),
        ],
        compiler_params=pltpu.CompilerParams(
            collective_id=0, has_side_effects=True, vmem_limit_bytes=48 * 1024 * 1024
        ),
    )(mass_field, factor_one.T, factor_two, factor_four.T)
    return summed[:, : na * slab] / (rank_one * rank_two * rank_four)


def solution(mesh):
    in_specs = (P(None, "wa", "an", None), P(), P("wa", None), P())
    out_specs = P("an", None)
    return jax.shard_map(
        on_device, mesh=mesh, in_specs=in_specs, out_specs=out_specs, check_vma=False
    )
```

```python
import functools

import jax
import jax.numpy as jnp
from jax import lax
from jax.experimental import pallas as pl
from jax.experimental.pallas import tpu as pltpu
from jax.sharding import PartitionSpec as P

MESH = pl.DeviceIdType.MESH
F32 = jnp.float32
BF16 = jnp.bfloat16
LANES = 128
SUB = 8


def iota(shape, dim):
    return lax.broadcasted_iota(jnp.int32, shape, dim)


def split(x):
    hi = x.astype(BF16)
    return hi, (x - hi.astype(F32)).astype(BF16)


def dot(a, b):
    return jnp.dot(a, b, preferred_element_type=F32)


def dot_nt(a, b):
    return lax.dot_general(a, b, (((1,), (1,)), ((), ())), preferred_element_type=F32)


def one_hot(shape, row, column):
    return jnp.where(row(iota(shape, 0)) == column(iota(shape, 1)), 1.0, 0.0).astype(BF16)


def near_first(count):
    half = count // 2
    return sorted(range(1, count), key=lambda o: (abs(o - half), o))


def kernel(
    nw, na, chunks,
    x_hbm, f1t_hbm, f2_hbm, f4t_hbm, out_ref,
    f1t_ref, f2_ref, f4t_ref, small_sem, xbuf, a1, f1s, red, f2all, a2, mix, got, proj, rows, part, part_in, term, term_in,
    x_sem, f2_send, f2_recv, mix_send, mix_recv, row_send, row_recv, part_send, part_recv, term_send, term_recv,
):
    me = lax.axis_index("wa")
    mine = lax.axis_index("an")
    species, fibre, slab, first = x_hbm.shape
    rank_one = f1t_ref.shape[0]
    rank_two = f2_ref.shape[1]
    rank_four = f4t_ref.shape[0]
    halves = mix.shape[1]
    width = halves * LANES
    q_groups = rank_four * slab // width
    per = fibre // chunks
    all_fibre = nw * fibre
    kept = rank_two * SUB
    share = kept // na
    wa_offsets = near_first(nw)
    an_offsets = near_first(na)

    def wa_peer(o):
        return lax.rem(me + o, nw)

    def an_peer(o):
        return lax.rem(mine + o, na)

    small = [
        pltpu.make_async_copy(src, dst, small_sem.at[n])
        for n, (src, dst) in enumerate(((f4t_hbm, f4t_ref), (f1t_hbm, f1t_ref), (f2_hbm, f2_ref)))
    ]
    for copy in small:
        copy.start()

    def load(j):
        return pltpu.make_async_copy(x_hbm.at[:, j], xbuf.at[j], x_sem.at[j])

    def start_load(j, carry):
        load(j).start()
        return carry

    lax.fori_loop(0, fibre, start_load, 0)

    barrier = pltpu.get_barrier_semaphore()
    for o in wa_offsets:
        pl.semaphore_signal(barrier, inc=1, device_id=(wa_peer(o), mine), device_id_type=MESH)
    for o in an_offsets:
        pl.semaphore_signal(barrier, inc=1, device_id=(me, an_peer(o)), device_id_type=MESH)

    for copy in small:
        copy.wait()
    f4hi, f4lo = split(f4t_ref[...])
    n1 = rank_four * SUB
    spread = one_hot((n1, rank_four), lambda r: r >> 3, lambda c: c)
    widen = one_hot((species, species * SUB), lambda r: r, lambda c: c >> 3)
    same = (iota((n1, species * SUB), 0) & 7) == (iota((n1, species * SUB), 1) & 7)
    for half, part4 in enumerate((f4hi, f4lo)):
        full = dot(dot(spread, part4).astype(BF16), widen)
        a1[half * n1 : (half + 1) * n1, :] = jnp.where(same, full, 0.0).astype(BF16)
    f1hi, f1lo = split(f1t_ref[...])
    f1s[:rank_one, :] = f1hi
    f1s[rank_one:, :] = f1lo
    f2all[me] = f2_ref[...]

    pl.semaphore_wait(barrier, nw + na - 2)

    def f2_copy(o):
        return pltpu.make_async_remote_copy(
            src_ref=f2all.at[me], dst_ref=f2all.at[me],
            send_sem=f2_send.at[o], recv_sem=f2_recv.at[o],
            device_id=(wa_peer(o), mine), device_id_type=MESH,
        )

    for o in wa_offsets:
        f2_copy(o).start()

    def mix_copy(c, h, o):
        peer = wa_peer(o)
        return pltpu.make_async_remote_copy(
            src_ref=mix.at[c, h, peer], dst_ref=got.at[c, h, me],
            send_sem=mix_send.at[c, h, o], recv_sem=mix_recv.at[c, h, o],
            device_id=(peer, mine), device_id_type=MESH,
        )

    def one_fibre(j, c, jj):
        for kh in range(slab // SUB):
            block = xbuf[j, :, kh * SUB : (kh + 1) * SUB, :].reshape(species * SUB, first)
            hi, lo = split(block)
            both = dot(a1[...], hi)
            reduced = both[:n1] + both[n1:] + dot(a1[:n1, :], lo)
            red[jj, :, kh * SUB : (kh + 1) * SUB, :] = reduced.reshape(rank_four, SUB, first)
        hi, lo = split(red[jj].reshape(rank_four * slab, first))
        both = dot_nt(f1s[...], hi)
        mixed = both[:rank_one] + both[rank_one:] + dot_nt(f1s[:rank_one, :], lo)
        for d in range(nw):
            rg, qg = d // q_groups, d % q_groups
            for h in range(halves):
                lane = qg * width + h * LANES
                mix[c, h, d, jj] = mixed[rg * SUB : (rg + 1) * SUB, lane : lane + LANES]

    def produce(c, carry):
        for jj in range(per):
            load(c * per + jj).wait()
            one_fibre(c * per + jj, c, jj)
        send(c, 0)
        for h in range(halves):
            got[c, h, me] = mix[c, h, me]
        return carry

    def send(c, h):
        for o in wa_offsets:
            mix_copy(c, h, o).start()

    def send_later(c, carry):
        for h in range(1, halves):
            send(c, h)
        return carry

    lax.fori_loop(0, chunks, produce, 0)
    if halves > 1:
        lax.fori_loop(0, chunks, send_later, 0)

    for o in wa_offsets:
        f2_copy(o).wait()
    f2hi, f2lo = split(f2all[...].reshape(all_fibre, rank_two))
    spread2 = one_hot((kept, rank_two), lambda r: r >> 3, lambda c: c)
    depth = nw * per * SUB
    same2 = (iota((kept, depth), 0) & 7) == (iota((kept, depth), 1) & 7)
    rows_hi = dot_nt(spread2, f2hi).astype(BF16)
    rows_lo = dot_nt(spread2, f2lo).astype(BF16)

    def expand(c, carry):
        def fibre_of(col):
            unit = col >> 3
            return (unit // per) * fibre + c * per + unit % per

        pick = one_hot((all_fibre, depth), lambda r: r, fibre_of)
        a2[c, :kept, :] = jnp.where(same2, dot(rows_hi, pick), 0.0).astype(BF16)
        a2[c, kept:, :] = jnp.where(same2, dot(rows_lo, pick), 0.0).astype(BF16)
        return carry

    lax.fori_loop(0, chunks, expand, 0)
    proj[...] = jnp.zeros_like(proj)

    def project(h):
        def add(c, carry):
            for o in wa_offsets:
                mix_copy(c, h, o).wait()
            hi, lo = split(got[c, h].reshape(depth, LANES))
            both = dot(a2[c], hi)
            proj[h] += both[:kept] + both[kept:] + dot(a2[c, :kept, :], lo)
            return carry

        lax.fori_loop(0, chunks, add, 0)

    def row_copy(h, o):
        peer = an_peer(o)
        return pltpu.make_async_remote_copy(
            src_ref=proj.at[h, pl.ds(pl.multiple_of(peer * share, SUB), share)], dst_ref=rows.at[h, mine],
            send_sem=row_send.at[h, o], recv_sem=row_recv.at[h, o],
            device_id=(me, peer), device_id_type=MESH,
        )

    q_row = iota((LANES, LANES), 0) // slab
    q_col = iota((LANES, LANES), 1) // slab
    lane_block = iota((na * slab, LANES), 1) // slab

    def gram_of(h):
        stack = jnp.concatenate([rows[h, a] for a in range(na)], axis=1)
        hi, lo = split(stack)
        thi, tlo = split(stack.T)
        total = jnp.zeros((na * slab, LANES), F32)
        for b in range(na):
            at = slice(b * LANES, (b + 1) * LANES)
            wide = dot(thi, hi[:, at]) + dot(thi, lo[:, at]) + dot(tlo, hi[:, at])
            wide = wide.reshape(na, LANES, LANES)
            wide = jnp.where((q_row == q_col)[None], wide, 0.0)
            wide = wide.reshape(na, LANES // slab, slab, LANES).sum(axis=1).reshape(na * slab, LANES)
            shift = LANES // 2
            while shift >= slab:
                wide = wide + pltpu.roll(wide, shift, 1)
                shift //= 2
            total = jnp.where(lane_block == b, wide, total)
        return total

    total = None
    for h in range(halves):
        project(h)
        for o in an_offsets:
            row_copy(h, o).start()
        rows[h, mine] = proj[h, pl.ds(pl.multiple_of(mine * share, SUB), share), :]
        for o in an_offsets:
            row_copy(h, o).wait()
        gram_half = gram_of(h)
        total = gram_half if total is None else total + gram_half
    part[...] = total.reshape(na, slab, LANES)

    def part_copy(o):
        peer = an_peer(o)
        return pltpu.make_async_remote_copy(
            src_ref=part.at[peer], dst_ref=part_in.at[mine],
            send_sem=part_send.at[o], recv_sem=part_recv.at[o],
            device_id=(me, peer), device_id_type=MESH,
        )

    for o in an_offsets:
        part_copy(o).start()
    part_in[mine] = part[mine]
    for o in an_offsets:
        part_copy(o).wait()
    term[...] = part_in[...].sum(axis=0)

    def term_copy(o):
        return pltpu.make_async_remote_copy(
            src_ref=term, dst_ref=term_in.at[me],
            send_sem=term_send.at[o], recv_sem=term_recv.at[o],
            device_id=(wa_peer(o), mine), device_id_type=MESH,
        )

    for o in wa_offsets:
        term_copy(o).start()
    term_in[me] = term[...]
    for o in wa_offsets:
        term_copy(o).wait()
    out_ref[...] = term_in[...].sum(axis=0)


def on_device(mass_field, factor_one, factor_two, factor_four):
    nw, na = lax.axis_size("wa"), lax.axis_size("an")
    species, fibre, slab, first = mass_field.shape
    rank_one, rank_two, rank_four = factor_one.shape[1], factor_two.shape[1], factor_four.shape[1]
    chunks = 4
    per = fibre // chunks
    halves = rank_one * rank_four * slab // (nw * SUB * LANES)
    kept = rank_two * SUB
    share = kept // na
    depth = nw * per * SUB
    dma = pltpu.SemaphoreType.DMA
    vmem = pl.BlockSpec(memory_space=pltpu.VMEM)
    summed = pl.pallas_call(
        functools.partial(kernel, nw, na, chunks),
        out_shape=jax.ShapeDtypeStruct((slab, LANES), F32),
        in_specs=[pl.BlockSpec(memory_space=pl.ANY)] * 4,
        out_specs=vmem,
        scratch_shapes=[
            pltpu.VMEM((rank_one, first), F32),
            pltpu.VMEM((fibre, rank_two), F32),
            pltpu.VMEM((rank_four, species), F32),
            dma((3,)),
            pltpu.VMEM((fibre, species, slab, first), F32),
            pltpu.VMEM((2 * rank_four * SUB, species * SUB), BF16),
            pltpu.VMEM((2 * rank_one, first), BF16),
            pltpu.VMEM((per, rank_four, slab, first), F32),
            pltpu.VMEM((nw, fibre, rank_two), F32),
            pltpu.VMEM((chunks, 2 * kept, depth), BF16),
            pltpu.VMEM((chunks, halves, nw, per, SUB, LANES), F32),
            pltpu.VMEM((chunks, halves, nw, per, SUB, LANES), F32),
            pltpu.VMEM((halves, kept, LANES), F32),
            pltpu.VMEM((halves, na, share, LANES), F32),
            pltpu.VMEM((na, slab, LANES), F32),
            pltpu.VMEM((na, slab, LANES), F32),
            pltpu.VMEM((slab, LANES), F32),
            pltpu.VMEM((nw, slab, LANES), F32),
            dma((fibre,)),
            dma((nw,)), dma((nw,)),
            dma((chunks, halves, nw)), dma((chunks, halves, nw)),
            dma((halves, na)), dma((halves, na)),
            dma((na,)), dma((na,)),
            dma((nw,)), dma((nw,)),
        ],
        compiler_params=pltpu.CompilerParams(
            collective_id=0, has_side_effects=True, vmem_limit_bytes=56 * 1024 * 1024
        ),
    )(mass_field, factor_one.T, factor_two, factor_four.T)
    return summed[:, : na * slab] / (rank_one * rank_two * rank_four)


def solution(mesh):
    in_specs = (P(None, "wa", "an", None), P(), P("wa", None), P())
    out_specs = P("an", None)
    return jax.shard_map(
        on_device, mesh=mesh, in_specs=in_specs, out_specs=out_specs, check_vma=False
    )
```

```python
import functools

import jax
import jax.numpy as jnp
from jax import lax
from jax.experimental import pallas as pl
from jax.experimental.pallas import tpu as pltpu
from jax.sharding import PartitionSpec as P

MESH = pl.DeviceIdType.MESH
F32 = jnp.float32
BF16 = jnp.bfloat16
LANES = 128
SUB = 8


def iota(shape, dim):
    return lax.broadcasted_iota(jnp.int32, shape, dim)


def split(x):
    hi = x.astype(BF16)
    return hi, (x - hi.astype(F32)).astype(BF16)


def dot(a, b):
    return jnp.dot(a, b, preferred_element_type=F32)


def dot_nt(a, b):
    return lax.dot_general(a, b, (((1,), (1,)), ((), ())), preferred_element_type=F32)


def one_hot(shape, row, column):
    return jnp.where(row(iota(shape, 0)) == column(iota(shape, 1)), 1.0, 0.0).astype(BF16)


def near_first(count):
    half = count // 2
    return sorted(range(1, count), key=lambda o: (abs(o - half), o))


def kernel(
    nw, na, chunks,
    x_hbm, f1t_hbm, f2_hbm, f4t_hbm, out_ref,
    f1t_ref, f2_ref, f4t_ref, small_sem, xbuf, a1, f1s, red, f2all, a2, mix, got, proj, rows, part, part_in, term, term_in,
    x_sem, f2_send, f2_recv, mix_send, mix_recv, row_send, row_recv, part_send, part_recv, term_send, term_recv,
):
    me = lax.axis_index("wa")
    mine = lax.axis_index("an")
    species, fibre, slab, first = x_hbm.shape
    rank_one = f1t_ref.shape[0]
    rank_two = f2_ref.shape[1]
    rank_four = f4t_ref.shape[0]
    halves = mix.shape[1]
    width = halves * LANES
    q_groups = rank_four * slab // width
    per = fibre // chunks
    all_fibre = nw * fibre
    kept = rank_two * SUB
    share = kept // na
    wa_offsets = near_first(nw)
    an_offsets = near_first(na)

    def wa_peer(o):
        return lax.rem(me + o, nw)

    def an_peer(o):
        return lax.rem(mine + o, na)

    small = [
        pltpu.make_async_copy(src, dst, small_sem.at[n])
        for n, (src, dst) in enumerate(((f4t_hbm, f4t_ref), (f1t_hbm, f1t_ref), (f2_hbm, f2_ref)))
    ]
    for copy in small:
        copy.start()

    def load(j):
        return pltpu.make_async_copy(x_hbm.at[:, j], xbuf.at[j], x_sem.at[j])

    def start_load(j, carry):
        load(j).start()
        return carry

    lax.fori_loop(0, fibre, start_load, 0)

    barrier = pltpu.get_barrier_semaphore()
    for o in wa_offsets:
        pl.semaphore_signal(barrier, inc=1, device_id=(wa_peer(o), mine), device_id_type=MESH)
    for o in an_offsets:
        pl.semaphore_signal(barrier, inc=1, device_id=(me, an_peer(o)), device_id_type=MESH)

    for copy in small:
        copy.wait()
    f4hi, f4lo = split(f4t_ref[...])
    n1 = rank_four * SUB
    spread = one_hot((n1, rank_four), lambda r: r >> 3, lambda c: c)
    widen = one_hot((species, species * SUB), lambda r: r, lambda c: c >> 3)
    same = (iota((n1, species * SUB), 0) & 7) == (iota((n1, species * SUB), 1) & 7)
    for half, part4 in enumerate((f4hi, f4lo)):
        full = dot(dot(spread, part4).astype(BF16), widen)
        a1[half * n1 : (half + 1) * n1, :] = jnp.where(same, full, 0.0).astype(BF16)
    f1hi, f1lo = split(f1t_ref[...])
    f1s[:rank_one, :] = f1hi
    f1s[rank_one:, :] = f1lo
    f2all[me] = f2_ref[...]

    pl.semaphore_wait(barrier, nw + na - 2)

    def f2_copy(o):
        return pltpu.make_async_remote_copy(
            src_ref=f2all.at[me], dst_ref=f2all.at[me],
            send_sem=f2_send.at[o], recv_sem=f2_recv.at[o],
            device_id=(wa_peer(o), mine), device_id_type=MESH,
        )

    for o in wa_offsets:
        f2_copy(o).start()

    def mix_copy(c, h, o):
        peer = wa_peer(o)
        return pltpu.make_async_remote_copy(
            src_ref=mix.at[c, h, peer], dst_ref=got.at[c, h, me],
            send_sem=mix_send.at[c, h, o], recv_sem=mix_recv.at[c, h, o],
            device_id=(peer, mine), device_id_type=MESH,
        )

    def reduce_species(j, jj):
        for kh in range(slab // SUB):
            block = xbuf[j, :, kh * SUB : (kh + 1) * SUB, :].reshape(species * SUB, first)
            hi, lo = split(block)
            both = dot(a1[...], hi)
            reduced = both[:n1] + both[n1:] + dot(a1[:n1, :], lo)
            red[jj, :, kh * SUB : (kh + 1) * SUB, :] = reduced.reshape(rank_four, SUB, first)

    def mix_first(c, jj):
        hi, lo = split(red[jj].reshape(rank_four * slab, first))
        both = dot_nt(f1s[...], hi)
        mixed = both[:rank_one] + both[rank_one:] + dot_nt(f1s[:rank_one, :], lo)
        for d in range(nw):
            rg, qg = d // q_groups, d % q_groups
            for h in range(halves):
                lane = qg * width + h * LANES
                mix[c, h, d, jj] = mixed[rg * SUB : (rg + 1) * SUB, lane : lane + LANES]

    def produce(c, carry):
        for jj in range(per):
            load(c * per + jj).wait()
        for jj in range(per):
            reduce_species(c * per + jj, jj)
        for jj in range(per):
            mix_first(c, jj)
        send(c, 0)
        for h in range(halves):
            got[c, h, me] = mix[c, h, me]
        return carry

    def send(c, h):
        for o in wa_offsets:
            mix_copy(c, h, o).start()

    def send_rest(c):
        for h in range(1, halves):
            send(c, h)

    lag = chunks // 2
    lax.fori_loop(0, lag, produce, 0)

    def produce_and_send(c, carry):
        produce(c, carry)
        send_rest(c - lag)
        return carry

    lax.fori_loop(lag, chunks, produce_and_send, 0)
    for c in range(chunks - lag, chunks):
        send_rest(c)

    for o in wa_offsets:
        f2_copy(o).wait()
    f2hi, f2lo = split(f2all[...].reshape(all_fibre, rank_two))
    spread2 = one_hot((kept, rank_two), lambda r: r >> 3, lambda c: c)
    depth = nw * per * SUB
    same2 = (iota((kept, depth), 0) & 7) == (iota((kept, depth), 1) & 7)
    rows_hi = dot_nt(spread2, f2hi).astype(BF16)
    rows_lo = dot_nt(spread2, f2lo).astype(BF16)

    def expand(c, carry):
        def fibre_of(col):
            unit = col >> 3
            return (unit // per) * fibre + c * per + unit % per

        pick = one_hot((all_fibre, depth), lambda r: r, fibre_of)
        a2[c, :kept, :] = jnp.where(same2, dot(rows_hi, pick), 0.0).astype(BF16)
        a2[c, kept:, :] = jnp.where(same2, dot(rows_lo, pick), 0.0).astype(BF16)
        return carry

    lax.fori_loop(0, chunks, expand, 0)
    proj[...] = jnp.zeros_like(proj)

    def project(h):
        def add(c, carry):
            for o in wa_offsets:
                mix_copy(c, h, o).wait()
            hi, lo = split(got[c, h].reshape(depth, LANES))
            both = dot(a2[c], hi)
            proj[h] += both[:kept] + both[kept:] + dot(a2[c, :kept, :], lo)
            return carry

        lax.fori_loop(0, chunks, add, 0)

    def row_copy(h, o):
        peer = an_peer(o)
        return pltpu.make_async_remote_copy(
            src_ref=proj.at[h, pl.ds(pl.multiple_of(peer * share, SUB), share)], dst_ref=rows.at[h, mine],
            send_sem=row_send.at[h, o], recv_sem=row_recv.at[h, o],
            device_id=(me, peer), device_id_type=MESH,
        )

    q_row = iota((LANES, LANES), 0) // slab
    q_col = iota((LANES, LANES), 1) // slab
    lane_block = iota((na * slab, LANES), 1) // slab

    def gram_of(h):
        stack = jnp.concatenate([rows[h, a] for a in range(na)], axis=1)
        hi, lo = split(stack)
        thi, tlo = split(stack.T)
        total = jnp.zeros((na * slab, LANES), F32)
        for b in range(na):
            at = slice(b * LANES, (b + 1) * LANES)
            wide = dot(thi, hi[:, at]) + dot(thi, lo[:, at]) + dot(tlo, hi[:, at])
            wide = wide.reshape(na, LANES, LANES)
            wide = jnp.where((q_row == q_col)[None], wide, 0.0)
            wide = wide.reshape(na, LANES // slab, slab, LANES).sum(axis=1).reshape(na * slab, LANES)
            shift = LANES // 2
            while shift >= slab:
                wide = wide + pltpu.roll(wide, shift, 1)
                shift //= 2
            total = jnp.where(lane_block == b, wide, total)
        return total

    total = None
    for h in range(halves):
        project(h)
        for o in an_offsets:
            row_copy(h, o).start()
        rows[h, mine] = proj[h, pl.ds(pl.multiple_of(mine * share, SUB), share), :]
        for o in an_offsets:
            row_copy(h, o).wait()
        gram_half = gram_of(h)
        total = gram_half if total is None else total + gram_half
    part[...] = total.reshape(na, slab, LANES)

    def part_copy(o):
        peer = an_peer(o)
        return pltpu.make_async_remote_copy(
            src_ref=part.at[peer], dst_ref=part_in.at[mine],
            send_sem=part_send.at[o], recv_sem=part_recv.at[o],
            device_id=(me, peer), device_id_type=MESH,
        )

    for o in an_offsets:
        part_copy(o).start()
    part_in[mine] = part[mine]
    for o in an_offsets:
        part_copy(o).wait()
    term[...] = part_in[...].sum(axis=0)

    def term_copy(o):
        return pltpu.make_async_remote_copy(
            src_ref=term, dst_ref=term_in.at[me],
            send_sem=term_send.at[o], recv_sem=term_recv.at[o],
            device_id=(wa_peer(o), mine), device_id_type=MESH,
        )

    for o in wa_offsets:
        term_copy(o).start()
    term_in[me] = term[...]
    for o in wa_offsets:
        term_copy(o).wait()
    out_ref[...] = term_in[...].sum(axis=0)


def on_device(mass_field, factor_one, factor_two, factor_four):
    nw, na = lax.axis_size("wa"), lax.axis_size("an")
    species, fibre, slab, first = mass_field.shape
    rank_one, rank_two, rank_four = factor_one.shape[1], factor_two.shape[1], factor_four.shape[1]
    chunks = 4
    per = fibre // chunks
    halves = rank_one * rank_four * slab // (nw * SUB * LANES)
    kept = rank_two * SUB
    share = kept // na
    depth = nw * per * SUB
    dma = pltpu.SemaphoreType.DMA
    vmem = pl.BlockSpec(memory_space=pltpu.VMEM)
    summed = pl.pallas_call(
        functools.partial(kernel, nw, na, chunks),
        out_shape=jax.ShapeDtypeStruct((slab, LANES), F32),
        in_specs=[pl.BlockSpec(memory_space=pl.ANY)] * 4,
        out_specs=vmem,
        scratch_shapes=[
            pltpu.VMEM((rank_one, first), F32),
            pltpu.VMEM((fibre, rank_two), F32),
            pltpu.VMEM((rank_four, species), F32),
            dma((3,)),
            pltpu.VMEM((fibre, species, slab, first), F32),
            pltpu.VMEM((2 * rank_four * SUB, species * SUB), BF16),
            pltpu.VMEM((2 * rank_one, first), BF16),
            pltpu.VMEM((per, rank_four, slab, first), F32),
            pltpu.VMEM((nw, fibre, rank_two), F32),
            pltpu.VMEM((chunks, 2 * kept, depth), BF16),
            pltpu.VMEM((chunks, halves, nw, per, SUB, LANES), F32),
            pltpu.VMEM((chunks, halves, nw, per, SUB, LANES), F32),
            pltpu.VMEM((halves, kept, LANES), F32),
            pltpu.VMEM((halves, na, share, LANES), F32),
            pltpu.VMEM((na, slab, LANES), F32),
            pltpu.VMEM((na, slab, LANES), F32),
            pltpu.VMEM((slab, LANES), F32),
            pltpu.VMEM((nw, slab, LANES), F32),
            dma((fibre,)),
            dma((nw,)), dma((nw,)),
            dma((chunks, halves, nw)), dma((chunks, halves, nw)),
            dma((halves, na)), dma((halves, na)),
            dma((na,)), dma((na,)),
            dma((nw,)), dma((nw,)),
        ],
        compiler_params=pltpu.CompilerParams(
            collective_id=0, has_side_effects=True, vmem_limit_bytes=56 * 1024 * 1024
        ),
    )(mass_field, factor_one.T, factor_two, factor_four.T)
    return summed[:, : na * slab] / (rank_one * rank_two * rank_four)


def solution(mesh):
    in_specs = (P(None, "wa", "an", None), P(), P("wa", None), P())
    out_specs = P("an", None)
    return jax.shard_map(
        on_device, mesh=mesh, in_specs=in_specs, out_specs=out_specs, check_vma=False
    )
```

```python
import functools

import jax
import jax.numpy as jnp
from jax import lax
from jax.experimental import pallas as pl
from jax.experimental.pallas import tpu as pltpu
from jax.sharding import PartitionSpec as P

MESH = pl.DeviceIdType.MESH
F32 = jnp.float32
BF16 = jnp.bfloat16
LANES = 128
SUB = 8


def iota(shape, dim):
    return lax.broadcasted_iota(jnp.int32, shape, dim)


def split(x):
    hi = x.astype(BF16)
    return hi, (x - hi.astype(F32)).astype(BF16)


def dot(a, b):
    return jnp.dot(a, b, preferred_element_type=F32)


def dot_nt(a, b):
    return lax.dot_general(a, b, (((1,), (1,)), ((), ())), preferred_element_type=F32)


def one_hot(shape, row, column):
    return jnp.where(row(iota(shape, 0)) == column(iota(shape, 1)), 1.0, 0.0).astype(BF16)


def near_first(count):
    half = count // 2
    return sorted(range(1, count), key=lambda o: (abs(o - half), o))


def kernel(
    nw, na, chunks,
    x_hbm, f1t_hbm, f2_hbm, f4t_hbm, out_ref,
    f1t_ref, f2_ref, f4t_ref, small_sem, xbuf, a1, f1s, red, f2all, a2, mix, got, proj, rows, part, part_in, term, term_in,
    x_sem, f2_send, f2_recv, mix_send, mix_recv, row_send, row_recv, part_send, part_recv, term_send, term_recv,
):
    me = lax.axis_index("wa")
    mine = lax.axis_index("an")
    species, fibre, slab, first = x_hbm.shape
    rank_one = f1t_ref.shape[0]
    rank_two = f2_ref.shape[1]
    rank_four = f4t_ref.shape[0]
    halves = mix.shape[0]
    width = halves * LANES
    q_groups = rank_four * slab // width
    per = fibre // chunks
    all_fibre = nw * fibre
    kept = rank_two * SUB
    share = kept // na
    wa_offsets = near_first(nw)
    an_offsets = near_first(na)

    def wa_peer(o):
        return lax.rem(me + o, nw)

    def an_peer(o):
        return lax.rem(mine + o, na)

    small = [
        pltpu.make_async_copy(src, dst, small_sem.at[n])
        for n, (src, dst) in enumerate(((f4t_hbm, f4t_ref), (f1t_hbm, f1t_ref), (f2_hbm, f2_ref)))
    ]
    for copy in small:
        copy.start()

    def load(j):
        return pltpu.make_async_copy(x_hbm.at[:, j], xbuf.at[j], x_sem.at[j])

    def start_load(j, carry):
        load(j).start()
        return carry

    lax.fori_loop(0, fibre, start_load, 0)

    barrier = pltpu.get_barrier_semaphore()
    for o in wa_offsets:
        pl.semaphore_signal(barrier, inc=1, device_id=(wa_peer(o), mine), device_id_type=MESH)
    for o in an_offsets:
        pl.semaphore_signal(barrier, inc=1, device_id=(me, an_peer(o)), device_id_type=MESH)

    for copy in small:
        copy.wait()
    f4hi, f4lo = split(f4t_ref[...])
    n1 = rank_four * SUB
    spread = one_hot((n1, rank_four), lambda r: r >> 3, lambda c: c)
    widen = one_hot((species, species * SUB), lambda r: r, lambda c: c >> 3)
    same = (iota((n1, species * SUB), 0) & 7) == (iota((n1, species * SUB), 1) & 7)
    for half, part4 in enumerate((f4hi, f4lo)):
        full = dot(dot(spread, part4).astype(BF16), widen)
        a1[half * n1 : (half + 1) * n1, :] = jnp.where(same, full, 0.0).astype(BF16)
    f1hi, f1lo = split(f1t_ref[...])
    f1s[:rank_one, :] = f1hi
    f1s[rank_one:, :] = f1lo
    f2all[me] = f2_ref[...]

    def f2_copy(o):
        return pltpu.make_async_remote_copy(
            src_ref=f2all.at[me], dst_ref=f2all.at[me],
            send_sem=f2_send.at[o], recv_sem=f2_recv.at[o],
            device_id=(wa_peer(o), mine), device_id_type=MESH,
        )

    def mix_copy(c, h, o):
        peer = wa_peer(o)
        span = pl.ds(c, 1 if h == 0 else 2)
        return pltpu.make_async_remote_copy(
            src_ref=mix.at[h, peer, span], dst_ref=got.at[h, me, span],
            send_sem=mix_send.at[c, h, o], recv_sem=mix_recv.at[c, h, o],
            device_id=(peer, mine), device_id_type=MESH,
        )

    def one_fibre(j, c, jj):
        for kh in range(slab // SUB):
            block = xbuf[j, :, kh * SUB : (kh + 1) * SUB, :].reshape(species * SUB, first)
            hi, lo = split(block)
            both = dot(a1[...], hi)
            reduced = both[:n1] + both[n1:] + dot(a1[:n1, :], lo)
            red[jj, :, kh * SUB : (kh + 1) * SUB, :] = reduced.reshape(rank_four, SUB, first)
        hi, lo = split(red[jj].reshape(rank_four * slab, first))
        both = dot_nt(f1s[...], hi)
        mixed = both[:rank_one] + both[rank_one:] + dot_nt(f1s[:rank_one, :], lo)
        for d in range(nw):
            rg, qg = d // q_groups, d % q_groups
            for h in range(halves):
                lane = qg * width + h * LANES
                mix[h, d, c, jj] = mixed[rg * SUB : (rg + 1) * SUB, lane : lane + LANES]

    def compute(c):
        for jj in range(per):
            load(c * per + jj).wait()
            one_fibre(c * per + jj, c, jj)
        for h in range(halves):
            got[h, me, c] = mix[h, me, c]

    def produce(c, carry):
        compute(c)
        send(c, 0)
        return carry

    def send(c, h):
        for o in wa_offsets:
            mix_copy(c, h, o).start()

    compute(0)
    pl.semaphore_wait(barrier, nw + na - 2)
    send(0, 0)
    for o in wa_offsets:
        f2_copy(o).start()
    lax.fori_loop(1, chunks, produce, 0)
    for h in range(1, halves):
        for c in range(0, chunks, 2):
            send(c, h)

    for o in wa_offsets:
        f2_copy(o).wait()
    f2hi, f2lo = split(f2all[...].reshape(all_fibre, rank_two))
    spread2 = one_hot((kept, rank_two), lambda r: r >> 3, lambda c: c)
    depth = nw * per * SUB
    same2 = (iota((kept, depth), 0) & 7) == (iota((kept, depth), 1) & 7)
    rows_hi = dot_nt(spread2, f2hi).astype(BF16)
    rows_lo = dot_nt(spread2, f2lo).astype(BF16)

    def expand(c, carry):
        def fibre_of(col):
            unit = col >> 3
            return (unit // per) * fibre + c * per + unit % per

        pick = one_hot((all_fibre, depth), lambda r: r, fibre_of)
        a2[c, :kept, :] = jnp.where(same2, dot(rows_hi, pick), 0.0).astype(BF16)
        a2[c, kept:, :] = jnp.where(same2, dot(rows_lo, pick), 0.0).astype(BF16)
        return carry

    lax.fori_loop(0, chunks, expand, 0)
    proj[...] = jnp.zeros_like(proj)

    def project(h):
        def add(c):
            hi, lo = split(got[h, :, c].reshape(depth, LANES))
            both = dot(a2[c], hi)
            proj[h] += both[:kept] + both[kept:] + dot(a2[c, :kept, :], lo)

        step = 1 if h == 0 else 2

        def group(g, carry):
            for o in wa_offsets:
                mix_copy(g * step, h, o).wait()
            for n in range(step):
                add(g * step + n)
            return carry

        lax.fori_loop(0, chunks // step, group, 0)

    def row_copy(h, o):
        peer = an_peer(o)
        return pltpu.make_async_remote_copy(
            src_ref=proj.at[h, pl.ds(pl.multiple_of(peer * share, SUB), share)], dst_ref=rows.at[h, mine],
            send_sem=row_send.at[h, o], recv_sem=row_recv.at[h, o],
            device_id=(me, peer), device_id_type=MESH,
        )

    q_row = iota((LANES, LANES), 0) // slab
    q_col = iota((LANES, LANES), 1) // slab
    lane_block = iota((na * slab, LANES), 1) // slab

    def gram_of(h):
        stack = jnp.concatenate([rows[h, a] for a in range(na)], axis=1)
        hi, lo = split(stack)
        thi, tlo = split(stack.T)
        total = jnp.zeros((na * slab, LANES), F32)
        for b in range(na):
            at = slice(b * LANES, (b + 1) * LANES)
            wide = dot(thi, hi[:, at]) + dot(thi, lo[:, at]) + dot(tlo, hi[:, at])
            wide = wide.reshape(na, LANES, LANES)
            wide = jnp.where((q_row == q_col)[None], wide, 0.0)
            wide = wide.reshape(na, LANES // slab, slab, LANES).sum(axis=1).reshape(na * slab, LANES)
            shift = LANES // 2
            while shift >= slab:
                wide = wide + pltpu.roll(wide, shift, 1)
                shift //= 2
            total = jnp.where(lane_block == b, wide, total)
        return total

    total = None
    for h in range(halves):
        project(h)
        for o in an_offsets:
            row_copy(h, o).start()
        rows[h, mine] = proj[h, pl.ds(pl.multiple_of(mine * share, SUB), share), :]
        for o in an_offsets:
            row_copy(h, o).wait()
        gram_half = gram_of(h)
        total = gram_half if total is None else total + gram_half
    part[...] = total.reshape(na, slab, LANES)

    def part_copy(o):
        peer = an_peer(o)
        return pltpu.make_async_remote_copy(
            src_ref=part.at[peer], dst_ref=part_in.at[mine],
            send_sem=part_send.at[o], recv_sem=part_recv.at[o],
            device_id=(me, peer), device_id_type=MESH,
        )

    for o in an_offsets:
        part_copy(o).start()
    part_in[mine] = part[mine]
    for o in an_offsets:
        part_copy(o).wait()
    term[...] = part_in[...].sum(axis=0)

    def term_copy(o):
        return pltpu.make_async_remote_copy(
            src_ref=term, dst_ref=term_in.at[me],
            send_sem=term_send.at[o], recv_sem=term_recv.at[o],
            device_id=(wa_peer(o), mine), device_id_type=MESH,
        )

    for o in wa_offsets:
        term_copy(o).start()
    term_in[me] = term[...]
    for o in wa_offsets:
        term_copy(o).wait()
    out_ref[...] = term_in[...].sum(axis=0)


def on_device(mass_field, factor_one, factor_two, factor_four):
    nw, na = lax.axis_size("wa"), lax.axis_size("an")
    species, fibre, slab, first = mass_field.shape
    rank_one, rank_two, rank_four = factor_one.shape[1], factor_two.shape[1], factor_four.shape[1]
    chunks = 4
    per = fibre // chunks
    halves = rank_one * rank_four * slab // (nw * SUB * LANES)
    kept = rank_two * SUB
    share = kept // na
    depth = nw * per * SUB
    dma = pltpu.SemaphoreType.DMA
    vmem = pl.BlockSpec(memory_space=pltpu.VMEM)
    summed = pl.pallas_call(
        functools.partial(kernel, nw, na, chunks),
        out_shape=jax.ShapeDtypeStruct((slab, LANES), F32),
        in_specs=[pl.BlockSpec(memory_space=pl.ANY)] * 4,
        out_specs=vmem,
        scratch_shapes=[
            pltpu.VMEM((rank_one, first), F32),
            pltpu.VMEM((fibre, rank_two), F32),
            pltpu.VMEM((rank_four, species), F32),
            dma((3,)),
            pltpu.VMEM((fibre, species, slab, first), F32),
            pltpu.VMEM((2 * rank_four * SUB, species * SUB), BF16),
            pltpu.VMEM((2 * rank_one, first), BF16),
            pltpu.VMEM((per, rank_four, slab, first), F32),
            pltpu.VMEM((nw, fibre, rank_two), F32),
            pltpu.VMEM((chunks, 2 * kept, depth), BF16),
            pltpu.VMEM((halves, nw, chunks, per, SUB, LANES), F32),
            pltpu.VMEM((halves, nw, chunks, per, SUB, LANES), F32),
            pltpu.VMEM((halves, kept, LANES), F32),
            pltpu.VMEM((halves, na, share, LANES), F32),
            pltpu.VMEM((na, slab, LANES), F32),
            pltpu.VMEM((na, slab, LANES), F32),
            pltpu.VMEM((slab, LANES), F32),
            pltpu.VMEM((nw, slab, LANES), F32),
            dma((fibre,)),
            dma((nw,)), dma((nw,)),
            dma((chunks, halves, nw)), dma((chunks, halves, nw)),
            dma((halves, na)), dma((halves, na)),
            dma((na,)), dma((na,)),
            dma((nw,)), dma((nw,)),
        ],
        compiler_params=pltpu.CompilerParams(
            collective_id=0, has_side_effects=True, vmem_limit_bytes=56 * 1024 * 1024
        ),
    )(mass_field, factor_one.T, factor_two, factor_four.T)
    return summed[:, : na * slab] / (rank_one * rank_two * rank_four)


def solution(mesh):
    in_specs = (P(None, "wa", "an", None), P(), P("wa", None), P())
    out_specs = P("an", None)
    return jax.shard_map(
        on_device, mesh=mesh, in_specs=in_specs, out_specs=out_specs, check_vma=False
    )
```

```python
import functools

import jax
import jax.numpy as jnp
from jax import lax
from jax.experimental import pallas as pl
from jax.experimental.pallas import tpu as pltpu
from jax.sharding import PartitionSpec as P

MESH = pl.DeviceIdType.MESH
F32 = jnp.float32
BF16 = jnp.bfloat16
LANES = 128
SUB = 8


def iota(shape, dim):
    return lax.broadcasted_iota(jnp.int32, shape, dim)


def split(x):
    hi = x.astype(BF16)
    return hi, (x - hi.astype(F32)).astype(BF16)


def dot(a, b):
    return jnp.dot(a, b, preferred_element_type=F32)


def dot_nt(a, b):
    return lax.dot_general(a, b, (((1,), (1,)), ((), ())), preferred_element_type=F32)


def one_hot(shape, row, column):
    return jnp.where(row(iota(shape, 0)) == column(iota(shape, 1)), 1.0, 0.0).astype(BF16)


def near_first(count):
    half = count // 2
    return sorted(range(1, count), key=lambda o: (abs(o - half), o))


def kernel(
    nw, na, chunks,
    x_hbm, f1t_hbm, f2_hbm, f4t_hbm, out_ref,
    f1t_ref, f2_ref, f4t_ref, small_sem, xbuf, a1, f1s, red, f2all, a2, mix, got, proj, rows, part, part_in, term, term_in,
    x_sem, f2_send, f2_recv, mix_send, mix_recv, row_send, row_recv, part_send, part_recv, term_send, term_recv,
):
    me = lax.axis_index("wa")
    mine = lax.axis_index("an")
    species, fibre, slab, first = x_hbm.shape
    rank_one = f1t_ref.shape[0]
    rank_two = f2_ref.shape[1]
    rank_four = f4t_ref.shape[0]
    halves = mix.shape[1]
    width = halves * LANES
    q_groups = rank_four * slab // width
    per = fibre // chunks
    all_fibre = nw * fibre
    kept = rank_two * SUB
    share = kept // na
    wa_offsets = near_first(nw)
    an_offsets = near_first(na)

    def wa_peer(o):
        return lax.rem(me + o, nw)

    def an_peer(o):
        return lax.rem(mine + o, na)

    small = [
        pltpu.make_async_copy(src, dst, small_sem.at[n])
        for n, (src, dst) in enumerate(((f4t_hbm, f4t_ref), (f1t_hbm, f1t_ref), (f2_hbm, f2_ref)))
    ]
    for copy in small:
        copy.start()

    def load(j):
        return pltpu.make_async_copy(x_hbm.at[:, j], xbuf.at[j], x_sem.at[j])

    def start_load(j, carry):
        load(j).start()
        return carry

    lax.fori_loop(0, fibre, start_load, 0)

    barrier = pltpu.get_barrier_semaphore()
    for o in wa_offsets:
        pl.semaphore_signal(barrier, inc=1, device_id=(wa_peer(o), mine), device_id_type=MESH)
    for o in an_offsets:
        pl.semaphore_signal(barrier, inc=1, device_id=(me, an_peer(o)), device_id_type=MESH)

    for copy in small:
        copy.wait()
    f4hi, f4lo = split(f4t_ref[...])
    n1 = rank_four * SUB
    spread = one_hot((n1, rank_four), lambda r: r >> 3, lambda c: c)
    widen = one_hot((species, species * SUB), lambda r: r, lambda c: c >> 3)
    same = (iota((n1, species * SUB), 0) & 7) == (iota((n1, species * SUB), 1) & 7)
    for half, part4 in enumerate((f4hi, f4lo)):
        full = dot(dot(spread, part4).astype(BF16), widen)
        a1[half * n1 : (half + 1) * n1, :] = jnp.where(same, full, 0.0).astype(BF16)
    f1hi, f1lo = split(f1t_ref[...])
    f1s[:rank_one, :] = f1hi
    f1s[rank_one:, :] = f1lo
    f2all[me] = f2_ref[...]

    pl.semaphore_wait(barrier, nw + na - 2)

    def f2_copy(o):
        return pltpu.make_async_remote_copy(
            src_ref=f2all.at[me], dst_ref=f2all.at[me],
            send_sem=f2_send.at[o], recv_sem=f2_recv.at[o],
            device_id=(wa_peer(o), mine), device_id_type=MESH,
        )

    for o in wa_offsets:
        f2_copy(o).start()

    def mix_copy(c, h, o):
        peer = wa_peer(o)
        return pltpu.make_async_remote_copy(
            src_ref=mix.at[c, h, peer], dst_ref=got.at[c, h, me],
            send_sem=mix_send.at[c, h, o], recv_sem=mix_recv.at[c, h, o],
            device_id=(peer, mine), device_id_type=MESH,
        )

    def one_fibre(j, c, jj):
        for kh in range(slab // SUB):
            block = xbuf[j, :, kh * SUB : (kh + 1) * SUB, :].reshape(species * SUB, first)
            hi, lo = split(block)
            both = dot(a1[...], hi)
            reduced = both[:n1] + both[n1:] + dot(a1[:n1, :], lo)
            red[jj, :, kh * SUB : (kh + 1) * SUB, :] = reduced.reshape(rank_four, SUB, first)
        hi, lo = split(red[jj].reshape(rank_four * slab, first))
        both = dot_nt(f1s[...], hi)
        mixed = both[:rank_one] + both[rank_one:] + dot_nt(f1s[:rank_one, :], lo)
        for d in range(nw):
            rg, qg = d // q_groups, d % q_groups
            for h in range(halves):
                lane = qg * width + h * LANES
                mix[c, h, d, jj] = mixed[rg * SUB : (rg + 1) * SUB, lane : lane + LANES]

    def produce(c, carry):
        for jj in range(per):
            load(c * per + jj).wait()
            one_fibre(c * per + jj, c, jj)
        send(c, 0)
        for h in range(halves):
            got[c, h, me] = mix[c, h, me]
        return carry

    def send(c, h):
        for o in wa_offsets:
            mix_copy(c, h, o).start()

    def send_later(c, carry):
        for h in range(1, halves):
            send(c, h)
        return carry

    lax.fori_loop(0, chunks, produce, 0)
    if halves > 1:
        lax.fori_loop(0, chunks, send_later, 0)

    for o in wa_offsets:
        f2_copy(o).wait()
    f2hi, f2lo = split(f2all[...].reshape(all_fibre, rank_two))
    spread2 = one_hot((kept, rank_two), lambda r: r >> 3, lambda c: c)
    depth = nw * per * SUB
    same2 = (iota((kept, depth), 0) & 7) == (iota((kept, depth), 1) & 7)
    rows_hi = dot_nt(spread2, f2hi).astype(BF16)
    rows_lo = dot_nt(spread2, f2lo).astype(BF16)

    def expand(c, carry):
        def fibre_of(col):
            unit = col >> 3
            return (unit // per) * fibre + c * per + unit % per

        pick = one_hot((all_fibre, depth), lambda r: r, fibre_of)
        a2[c, :kept, :] = jnp.where(same2, dot(rows_hi, pick), 0.0).astype(BF16)
        a2[c, kept:, :] = jnp.where(same2, dot(rows_lo, pick), 0.0).astype(BF16)
        return carry

    lax.fori_loop(0, chunks, expand, 0)
    proj[...] = jnp.zeros_like(proj)

    def project(h):
        def add(c, carry):
            for o in wa_offsets:
                mix_copy(c, h, o).wait()
            hi, lo = split(got[c, h].reshape(depth, LANES))
            both = dot(a2[c], hi)
            proj[h] += both[:kept] + both[kept:] + dot(a2[c, :kept, :], lo)
            return carry

        lax.fori_loop(0, chunks, add, 0)

    def row_copy(h, o):
        peer = an_peer(o)
        return pltpu.make_async_remote_copy(
            src_ref=proj.at[h, pl.ds(pl.multiple_of(peer * share, SUB), share)], dst_ref=rows.at[h, mine],
            send_sem=row_send.at[h, o], recv_sem=row_recv.at[h, o],
            device_id=(me, peer), device_id_type=MESH,
        )

    q_row = iota((LANES, LANES), 0) // slab
    q_col = iota((LANES, LANES), 1) // slab
    lane_block = iota((na * slab, LANES), 1) // slab

    def gram_of(h):
        stack = jnp.concatenate([rows[h, a] for a in range(na)], axis=1)
        hi, lo = split(stack)
        thi, tlo = split(stack.T)
        total = jnp.zeros((na * slab, LANES), F32)
        for b in range(na):
            at = slice(b * LANES, (b + 1) * LANES)
            wide = dot(thi, hi[:, at]) + dot(thi, lo[:, at]) + dot(tlo, hi[:, at])
            wide = wide.reshape(na, LANES, LANES)
            wide = jnp.where((q_row == q_col)[None], wide, 0.0)
            wide = wide.reshape(na, LANES // slab, slab, LANES).sum(axis=1).reshape(na * slab, LANES)
            shift = LANES // 2
            while shift >= slab:
                wide = wide + pltpu.roll(wide, shift, 1)
                shift //= 2
            total = jnp.where(lane_block == b, wide, total)
        return total

    total = None
    for h in range(halves):
        project(h)
        for o in an_offsets:
            row_copy(h, o).start()
        rows[h, mine] = proj[h, pl.ds(pl.multiple_of(mine * share, SUB), share), :]
        for o in an_offsets:
            row_copy(h, o).wait()
        gram_half = gram_of(h)
        total = gram_half if total is None else total + gram_half
    part[...] = total.reshape(na, slab, LANES)

    def part_copy(o):
        peer = an_peer(o)
        return pltpu.make_async_remote_copy(
            src_ref=part.at[peer], dst_ref=part_in.at[mine],
            send_sem=part_send.at[o], recv_sem=part_recv.at[o],
            device_id=(me, peer), device_id_type=MESH,
        )

    for o in an_offsets:
        part_copy(o).start()
    part_in[mine] = part[mine]
    for o in an_offsets:
        part_copy(o).wait()
    term[...] = part_in[...].sum(axis=0)

    def term_copy(o):
        return pltpu.make_async_remote_copy(
            src_ref=term, dst_ref=term_in.at[me],
            send_sem=term_send.at[o], recv_sem=term_recv.at[o],
            device_id=(wa_peer(o), mine), device_id_type=MESH,
        )

    for o in wa_offsets:
        term_copy(o).start()
    term_in[me] = term[...]
    for o in wa_offsets:
        term_copy(o).wait()
    out_ref[...] = term_in[...].sum(axis=0)


def on_device(mass_field, factor_one, factor_two, factor_four):
    nw, na = lax.axis_size("wa"), lax.axis_size("an")
    species, fibre, slab, first = mass_field.shape
    rank_one, rank_two, rank_four = factor_one.shape[1], factor_two.shape[1], factor_four.shape[1]
    chunks = 8
    per = fibre // chunks
    halves = rank_one * rank_four * slab // (nw * SUB * LANES)
    kept = rank_two * SUB
    share = kept // na
    depth = nw * per * SUB
    dma = pltpu.SemaphoreType.DMA
    vmem = pl.BlockSpec(memory_space=pltpu.VMEM)
    summed = pl.pallas_call(
        functools.partial(kernel, nw, na, chunks),
        out_shape=jax.ShapeDtypeStruct((slab, LANES), F32),
        in_specs=[pl.BlockSpec(memory_space=pl.ANY)] * 4,
        out_specs=vmem,
        scratch_shapes=[
            pltpu.VMEM((rank_one, first), F32),
            pltpu.VMEM((fibre, rank_two), F32),
            pltpu.VMEM((rank_four, species), F32),
            dma((3,)),
            pltpu.VMEM((fibre, species, slab, first), F32),
            pltpu.VMEM((2 * rank_four * SUB, species * SUB), BF16),
            pltpu.VMEM((2 * rank_one, first), BF16),
            pltpu.VMEM((per, rank_four, slab, first), F32),
            pltpu.VMEM((nw, fibre, rank_two), F32),
            pltpu.VMEM((chunks, 2 * kept, depth), BF16),
            pltpu.VMEM((chunks, halves, nw, per, SUB, LANES), F32),
            pltpu.VMEM((chunks, halves, nw, per, SUB, LANES), F32),
            pltpu.VMEM((halves, kept, LANES), F32),
            pltpu.VMEM((halves, na, share, LANES), F32),
            pltpu.VMEM((na, slab, LANES), F32),
            pltpu.VMEM((na, slab, LANES), F32),
            pltpu.VMEM((slab, LANES), F32),
            pltpu.VMEM((nw, slab, LANES), F32),
            dma((fibre,)),
            dma((nw,)), dma((nw,)),
            dma((chunks, halves, nw)), dma((chunks, halves, nw)),
            dma((halves, na)), dma((halves, na)),
            dma((na,)), dma((na,)),
            dma((nw,)), dma((nw,)),
        ],
        compiler_params=pltpu.CompilerParams(
            collective_id=0, has_side_effects=True, vmem_limit_bytes=56 * 1024 * 1024
        ),
    )(mass_field, factor_one.T, factor_two, factor_four.T)
    return summed[:, : na * slab] / (rank_one * rank_two * rank_four)


def solution(mesh):
    in_specs = (P(None, "wa", "an", None), P(), P("wa", None), P())
    out_specs = P("an", None)
    return jax.shard_map(
        on_device, mesh=mesh, in_specs=in_specs, out_specs=out_specs, check_vma=False
    )
```

```python
import functools

import jax
import jax.numpy as jnp
from jax import lax
from jax.experimental import pallas as pl
from jax.experimental.pallas import tpu as pltpu
from jax.sharding import PartitionSpec as P

MESH = pl.DeviceIdType.MESH
F32 = jnp.float32
BF16 = jnp.bfloat16
LANES = 128
SUB = 8


def iota(shape, dim):
    return lax.broadcasted_iota(jnp.int32, shape, dim)


def split(x):
    hi = x.astype(BF16)
    return hi, (x - hi.astype(F32)).astype(BF16)


def dot(a, b):
    return jnp.dot(a, b, preferred_element_type=F32)


def dot_nt(a, b):
    return lax.dot_general(a, b, (((1,), (1,)), ((), ())), preferred_element_type=F32)


def one_hot(shape, row, column):
    return jnp.where(row(iota(shape, 0)) == column(iota(shape, 1)), 1.0, 0.0).astype(BF16)


def near_first(count):
    half = count // 2
    return sorted(range(1, count), key=lambda o: (abs(o - half), o))


def kernel(
    nw, na, chunks,
    x_hbm, f1t_hbm, f2_hbm, f4t_hbm, out_ref,
    f1t_ref, f2_ref, f4t_ref, small_sem, xbuf, a1, f1s, red, f2all, a2, mix, got, proj, rows, part, part_in, term, term_in,
    x_sem, f2_send, f2_recv, mix_send, mix_recv, row_send, row_recv, part_send, part_recv, term_send, term_recv,
):
    me = lax.axis_index("wa")
    mine = lax.axis_index("an")
    species, fibre, slab, first = x_hbm.shape
    rank_one = f1t_ref.shape[0]
    rank_two = f2_ref.shape[1]
    rank_four = f4t_ref.shape[0]
    halves = mix.shape[1]
    width = halves * LANES
    q_groups = rank_four * slab // width
    per = fibre // chunks
    all_fibre = nw * fibre
    kept = rank_two * SUB
    share = kept // na
    wa_offsets = near_first(nw)
    an_offsets = near_first(na)

    def wa_peer(o):
        return lax.rem(me + o, nw)

    def an_peer(o):
        return lax.rem(mine + o, na)

    small = [
        pltpu.make_async_copy(src, dst, small_sem.at[n])
        for n, (src, dst) in enumerate(((f4t_hbm, f4t_ref), (f1t_hbm, f1t_ref), (f2_hbm, f2_ref)))
    ]
    for copy in small:
        copy.start()

    def load(j):
        return pltpu.make_async_copy(x_hbm.at[:, j], xbuf.at[j], x_sem.at[j])

    def start_load(j, carry):
        load(j).start()
        return carry

    lax.fori_loop(0, fibre, start_load, 0)

    barrier = pltpu.get_barrier_semaphore()
    for o in wa_offsets:
        pl.semaphore_signal(barrier, inc=1, device_id=(wa_peer(o), mine), device_id_type=MESH)
    for o in an_offsets:
        pl.semaphore_signal(barrier, inc=1, device_id=(me, an_peer(o)), device_id_type=MESH)

    for copy in small:
        copy.wait()
    f4hi, f4lo = split(f4t_ref[...])
    n1 = rank_four * SUB
    spread = one_hot((n1, rank_four), lambda r: r >> 3, lambda c: c)
    widen = one_hot((species, species * SUB), lambda r: r, lambda c: c >> 3)
    same = (iota((n1, species * SUB), 0) & 7) == (iota((n1, species * SUB), 1) & 7)
    for half, part4 in enumerate((f4hi, f4lo)):
        full = dot(dot(spread, part4).astype(BF16), widen)
        a1[half * n1 : (half + 1) * n1, :] = jnp.where(same, full, 0.0).astype(BF16)
    f1hi, f1lo = split(f1t_ref[...])
    f1s[:rank_one, :] = f1hi
    f1s[rank_one:, :] = f1lo
    f2all[me] = f2_ref[...]

    def f2_copy(o):
        return pltpu.make_async_remote_copy(
            src_ref=f2all.at[me], dst_ref=f2all.at[me],
            send_sem=f2_send.at[o], recv_sem=f2_recv.at[o],
            device_id=(wa_peer(o), mine), device_id_type=MESH,
        )

    def mix_copy(c, h, o):
        peer = wa_peer(o)
        return pltpu.make_async_remote_copy(
            src_ref=mix.at[c, h, peer], dst_ref=got.at[c, h, me],
            send_sem=mix_send.at[c, h, o], recv_sem=mix_recv.at[c, h, o],
            device_id=(peer, mine), device_id_type=MESH,
        )

    def one_fibre(j, c, jj):
        for kh in range(slab // SUB):
            block = xbuf[j, :, kh * SUB : (kh + 1) * SUB, :].reshape(species * SUB, first)
            hi, lo = split(block)
            both = dot(a1[...], hi)
            reduced = both[:n1] + both[n1:] + dot(a1[:n1, :], lo)
            red[jj, :, kh * SUB : (kh + 1) * SUB, :] = reduced.reshape(rank_four, SUB, first)
        hi, lo = split(red[jj].reshape(rank_four * slab, first))
        both = dot_nt(f1s[...], hi)
        mixed = both[:rank_one] + both[rank_one:] + dot_nt(f1s[:rank_one, :], lo)
        for d in range(nw):
            rg, qg = d // q_groups, d % q_groups
            for h in range(halves):
                lane = qg * width + h * LANES
                mix[c, h, d, jj] = mixed[rg * SUB : (rg + 1) * SUB, lane : lane + LANES]

    def compute(c):
        for jj in range(per):
            load(c * per + jj).wait()
            one_fibre(c * per + jj, c, jj)
        for h in range(halves):
            got[c, h, me] = mix[c, h, me]

    def produce(c, carry):
        compute(c)
        send(c, 0)
        return carry

    def send(c, h):
        for o in wa_offsets:
            mix_copy(c, h, o).start()

    def send_later(c, carry):
        for h in range(1, halves):
            send(c, h)
        return carry

    compute(0)
    pl.semaphore_wait(barrier, nw + na - 2)
    send(0, 0)
    for o in wa_offsets:
        f2_copy(o).start()
    lax.fori_loop(1, chunks, produce, 0)
    if halves > 1:
        lax.fori_loop(0, chunks, send_later, 0)

    for o in wa_offsets:
        f2_copy(o).wait()
    f2hi, f2lo = split(f2all[...].reshape(all_fibre, rank_two))
    spread2 = one_hot((kept, rank_two), lambda r: r >> 3, lambda c: c)
    depth = nw * per * SUB
    same2 = (iota((kept, depth), 0) & 7) == (iota((kept, depth), 1) & 7)
    rows_hi = dot_nt(spread2, f2hi).astype(BF16)
    rows_lo = dot_nt(spread2, f2lo).astype(BF16)

    def expand(c, carry):
        def fibre_of(col):
            unit = col >> 3
            return (unit // per) * fibre + c * per + unit % per

        pick = one_hot((all_fibre, depth), lambda r: r, fibre_of)
        a2[c, :kept, :] = jnp.where(same2, dot(rows_hi, pick), 0.0).astype(BF16)
        a2[c, kept:, :] = jnp.where(same2, dot(rows_lo, pick), 0.0).astype(BF16)
        return carry

    lax.fori_loop(0, chunks, expand, 0)
    proj[...] = jnp.zeros_like(proj)

    def project(h):
        def add(c, carry):
            for o in wa_offsets:
                mix_copy(c, h, o).wait()
            hi, lo = split(got[c, h].reshape(depth, LANES))
            both = dot(a2[c], hi)
            proj[h] += both[:kept] + both[kept:] + dot(a2[c, :kept, :], lo)
            return carry

        lax.fori_loop(0, chunks, add, 0)

    def row_copy(h, o):
        peer = an_peer(o)
        return pltpu.make_async_remote_copy(
            src_ref=proj.at[h, pl.ds(pl.multiple_of(peer * share, SUB), share)], dst_ref=rows.at[h, mine],
            send_sem=row_send.at[h, o], recv_sem=row_recv.at[h, o],
            device_id=(me, peer), device_id_type=MESH,
        )

    q_row = iota((LANES, LANES), 0) // slab
    q_col = iota((LANES, LANES), 1) // slab
    lane_block = iota((na * slab, LANES), 1) // slab

    def gram_of(h):
        stack = jnp.concatenate([rows[h, a] for a in range(na)], axis=1)
        hi, lo = split(stack)
        thi, tlo = split(stack.T)
        total = jnp.zeros((na * slab, LANES), F32)
        for b in range(na):
            at = slice(b * LANES, (b + 1) * LANES)
            wide = dot(thi, hi[:, at]) + dot(thi, lo[:, at]) + dot(tlo, hi[:, at])
            wide = wide.reshape(na, LANES, LANES)
            wide = jnp.where((q_row == q_col)[None], wide, 0.0)
            wide = wide.reshape(na, LANES // slab, slab, LANES).sum(axis=1).reshape(na * slab, LANES)
            shift = LANES // 2
            while shift >= slab:
                wide = wide + pltpu.roll(wide, shift, 1)
                shift //= 2
            total = jnp.where(lane_block == b, wide, total)
        return total

    for h in range(halves):
        project(h)
        for o in an_offsets:
            row_copy(h, o).start()
        rows[h, mine] = proj[h, pl.ds(pl.multiple_of(mine * share, SUB), share), :]

    total = None
    for h in range(halves):
        for o in an_offsets:
            row_copy(h, o).wait()
        gram_half = gram_of(h)
        total = gram_half if total is None else total + gram_half
    part[...] = total.reshape(na, slab, LANES)

    def part_copy(o):
        peer = an_peer(o)
        return pltpu.make_async_remote_copy(
            src_ref=part.at[peer], dst_ref=part_in.at[mine],
            send_sem=part_send.at[o], recv_sem=part_recv.at[o],
            device_id=(me, peer), device_id_type=MESH,
        )

    for o in an_offsets:
        part_copy(o).start()
    part_in[mine] = part[mine]
    for o in an_offsets:
        part_copy(o).wait()
    term[...] = part_in[...].sum(axis=0)

    def term_copy(o):
        return pltpu.make_async_remote_copy(
            src_ref=term, dst_ref=term_in.at[me],
            send_sem=term_send.at[o], recv_sem=term_recv.at[o],
            device_id=(wa_peer(o), mine), device_id_type=MESH,
        )

    for o in wa_offsets:
        term_copy(o).start()
    term_in[me] = term[...]
    for o in wa_offsets:
        term_copy(o).wait()
    out_ref[...] = term_in[...].sum(axis=0)


def on_device(mass_field, factor_one, factor_two, factor_four):
    nw, na = lax.axis_size("wa"), lax.axis_size("an")
    species, fibre, slab, first = mass_field.shape
    rank_one, rank_two, rank_four = factor_one.shape[1], factor_two.shape[1], factor_four.shape[1]
    chunks = 4
    per = fibre // chunks
    halves = rank_one * rank_four * slab // (nw * SUB * LANES)
    kept = rank_two * SUB
    share = kept // na
    depth = nw * per * SUB
    dma = pltpu.SemaphoreType.DMA
    vmem = pl.BlockSpec(memory_space=pltpu.VMEM)
    summed = pl.pallas_call(
        functools.partial(kernel, nw, na, chunks),
        out_shape=jax.ShapeDtypeStruct((slab, LANES), F32),
        in_specs=[pl.BlockSpec(memory_space=pl.ANY)] * 4,
        out_specs=vmem,
        scratch_shapes=[
            pltpu.VMEM((rank_one, first), F32),
            pltpu.VMEM((fibre, rank_two), F32),
            pltpu.VMEM((rank_four, species), F32),
            dma((3,)),
            pltpu.VMEM((fibre, species, slab, first), F32),
            pltpu.VMEM((2 * rank_four * SUB, species * SUB), BF16),
            pltpu.VMEM((2 * rank_one, first), BF16),
            pltpu.VMEM((per, rank_four, slab, first), F32),
            pltpu.VMEM((nw, fibre, rank_two), F32),
            pltpu.VMEM((chunks, 2 * kept, depth), BF16),
            pltpu.VMEM((chunks, halves, nw, per, SUB, LANES), F32),
            pltpu.VMEM((chunks, halves, nw, per, SUB, LANES), F32),
            pltpu.VMEM((halves, kept, LANES), F32),
            pltpu.VMEM((halves, na, share, LANES), F32),
            pltpu.VMEM((na, slab, LANES), F32),
            pltpu.VMEM((na, slab, LANES), F32),
            pltpu.VMEM((slab, LANES), F32),
            pltpu.VMEM((nw, slab, LANES), F32),
            dma((fibre,)),
            dma((nw,)), dma((nw,)),
            dma((chunks, halves, nw)), dma((chunks, halves, nw)),
            dma((halves, na)), dma((halves, na)),
            dma((na,)), dma((na,)),
            dma((nw,)), dma((nw,)),
        ],
        compiler_params=pltpu.CompilerParams(
            collective_id=0, has_side_effects=True, vmem_limit_bytes=56 * 1024 * 1024
        ),
    )(mass_field, factor_one.T, factor_two, factor_four.T)
    return summed[:, : na * slab] / (rank_one * rank_two * rank_four)


def solution(mesh):
    in_specs = (P(None, "wa", "an", None), P(), P("wa", None), P())
    out_specs = P("an", None)
    return jax.shard_map(
        on_device, mesh=mesh, in_specs=in_specs, out_specs=out_specs, check_vma=False
    )
```

```python
import functools

import jax
import jax.numpy as jnp
from jax import lax
from jax.experimental import pallas as pl
from jax.experimental.pallas import tpu as pltpu
from jax.sharding import PartitionSpec as P

MESH = pl.DeviceIdType.MESH
F32 = jnp.float32
BF16 = jnp.bfloat16
LANES = 128
SUB = 8


def iota(shape, dim):
    return lax.broadcasted_iota(jnp.int32, shape, dim)


def split(x):
    hi = x.astype(BF16)
    return hi, (x - hi.astype(F32)).astype(BF16)


def dot(a, b):
    return jnp.dot(a, b, preferred_element_type=F32)


def dot_nt(a, b):
    return lax.dot_general(a, b, (((1,), (1,)), ((), ())), preferred_element_type=F32)


def one_hot(shape, row, column):
    return jnp.where(row(iota(shape, 0)) == column(iota(shape, 1)), 1.0, 0.0).astype(BF16)


def near_first(count):
    half = count // 2
    return sorted(range(1, count), key=lambda o: (abs(o - half), o))


def kernel(
    nw, na, chunks,
    x_hbm, f1t_hbm, f2_hbm, f4t_hbm, out_ref,
    f1t_ref, f2_ref, f4t_ref, small_sem, xbuf, a1, f1s, red, f2all, a2, mix, got, proj, rows, part, part_in, term, term_in,
    x_sem, f2_send, f2_recv, mix_send, mix_recv, row_send, row_recv, part_send, part_recv, term_send, term_recv,
):
    me = lax.axis_index("wa")
    mine = lax.axis_index("an")
    species, fibre, slab, first = x_hbm.shape
    rank_one = f1t_ref.shape[0]
    rank_two = f2_ref.shape[1]
    rank_four = f4t_ref.shape[0]
    halves = mix.shape[1]
    width = halves * LANES
    q_groups = rank_four * slab // width
    per = fibre // chunks
    all_fibre = nw * fibre
    kept = rank_two * SUB
    share = kept // na
    wa_offsets = near_first(nw)
    an_offsets = near_first(na)

    def wa_peer(o):
        return lax.rem(me + o, nw)

    def an_peer(o):
        return lax.rem(mine + o, na)

    small = [
        pltpu.make_async_copy(src, dst, small_sem.at[n])
        for n, (src, dst) in enumerate(((f4t_hbm, f4t_ref), (f1t_hbm, f1t_ref), (f2_hbm, f2_ref)))
    ]
    for copy in small:
        copy.start()

    def load(j):
        return pltpu.make_async_copy(x_hbm.at[:, j], xbuf.at[j], x_sem.at[j])

    def start_load(j, carry):
        load(j).start()
        return carry

    lax.fori_loop(0, fibre, start_load, 0)

    barrier = pltpu.get_barrier_semaphore()
    for o in wa_offsets:
        pl.semaphore_signal(barrier, inc=1, device_id=(wa_peer(o), mine), device_id_type=MESH)
    for o in an_offsets:
        pl.semaphore_signal(barrier, inc=1, device_id=(me, an_peer(o)), device_id_type=MESH)

    for copy in small:
        copy.wait()
    f4hi, f4lo = split(f4t_ref[...])
    n1 = rank_four * SUB
    spread = one_hot((n1, rank_four), lambda r: r >> 3, lambda c: c)
    widen = one_hot((species, species * SUB), lambda r: r, lambda c: c >> 3)
    same = (iota((n1, species * SUB), 0) & 7) == (iota((n1, species * SUB), 1) & 7)
    deep = species * SUB
    for half, part4 in enumerate((f4hi, f4hi, f4lo)):
        full = dot(dot(spread, part4).astype(BF16), widen)
        a1[:, half * deep : (half + 1) * deep] = jnp.where(same, full, 0.0).astype(BF16)
    f1hi, f1lo = split(f1t_ref[...])
    f1s[...] = jnp.concatenate([f1hi, f1hi, f1lo], axis=1)
    f2all[me] = f2_ref[...]

    def f2_copy(o):
        return pltpu.make_async_remote_copy(
            src_ref=f2all.at[me], dst_ref=f2all.at[me],
            send_sem=f2_send.at[o], recv_sem=f2_recv.at[o],
            device_id=(wa_peer(o), mine), device_id_type=MESH,
        )

    def mix_copy(c, h, o):
        peer = wa_peer(o)
        return pltpu.make_async_remote_copy(
            src_ref=mix.at[c, h, peer], dst_ref=got.at[c, h, me],
            send_sem=mix_send.at[c, h, o], recv_sem=mix_recv.at[c, h, o],
            device_id=(peer, mine), device_id_type=MESH,
        )

    def one_fibre(j, c, jj):
        for kh in range(slab // SUB):
            block = xbuf[j, :, kh * SUB : (kh + 1) * SUB, :].reshape(species * SUB, first)
            hi, lo = split(block)
            reduced = dot(a1[...], jnp.concatenate([hi, lo, hi], axis=0))
            red[jj, :, kh * SUB : (kh + 1) * SUB, :] = reduced.reshape(rank_four, SUB, first)
        hi, lo = split(red[jj].reshape(rank_four * slab, first))
        mixed = dot_nt(f1s[...], jnp.concatenate([hi, lo, hi], axis=1))
        for d in range(nw):
            rg, qg = d // q_groups, d % q_groups
            for h in range(halves):
                lane = qg * width + h * LANES
                mix[c, h, d, jj] = mixed[rg * SUB : (rg + 1) * SUB, lane : lane + LANES]

    def compute(c):
        for jj in range(per):
            load(c * per + jj).wait()
            one_fibre(c * per + jj, c, jj)
        for h in range(halves):
            got[c, h, me] = mix[c, h, me]

    def produce(c, carry):
        compute(c)
        send(c, 0)
        return carry

    def send(c, h):
        for o in wa_offsets:
            mix_copy(c, h, o).start()

    def send_later(c, carry):
        for h in range(1, halves):
            send(c, h)
        return carry

    compute(0)
    pl.semaphore_wait(barrier, nw + na - 2)
    send(0, 0)
    for o in wa_offsets:
        f2_copy(o).start()
    lax.fori_loop(1, chunks, produce, 0)
    if halves > 1:
        lax.fori_loop(0, chunks, send_later, 0)

    for o in wa_offsets:
        f2_copy(o).wait()
    f2hi, f2lo = split(f2all[...].reshape(all_fibre, rank_two))
    spread2 = one_hot((kept, rank_two), lambda r: r >> 3, lambda c: c)
    depth = nw * per * SUB
    same2 = (iota((kept, depth), 0) & 7) == (iota((kept, depth), 1) & 7)
    rows_hi = dot_nt(spread2, f2hi).astype(BF16)
    rows_lo = dot_nt(spread2, f2lo).astype(BF16)

    def expand(c, carry):
        def fibre_of(col):
            unit = col >> 3
            return (unit // per) * fibre + c * per + unit % per

        pick = one_hot((all_fibre, depth), lambda r: r, fibre_of)
        a2[c, :kept, :] = jnp.where(same2, dot(rows_hi, pick), 0.0).astype(BF16)
        a2[c, kept:, :] = jnp.where(same2, dot(rows_lo, pick), 0.0).astype(BF16)
        return carry

    lax.fori_loop(0, chunks, expand, 0)
    proj[...] = jnp.zeros_like(proj)

    def project(h):
        def add(c, carry):
            for o in wa_offsets:
                mix_copy(c, h, o).wait()
            hi, lo = split(got[c, h].reshape(depth, LANES))
            both = dot(a2[c], hi)
            proj[h] += both[:kept] + both[kept:] + dot(a2[c, :kept, :], lo)
            return carry

        lax.fori_loop(0, chunks, add, 0)

    def row_copy(h, o):
        peer = an_peer(o)
        return pltpu.make_async_remote_copy(
            src_ref=proj.at[h, pl.ds(pl.multiple_of(peer * share, SUB), share)], dst_ref=rows.at[h, mine],
            send_sem=row_send.at[h, o], recv_sem=row_recv.at[h, o],
            device_id=(me, peer), device_id_type=MESH,
        )

    q_row = iota((LANES, LANES), 0) // slab
    q_col = iota((LANES, LANES), 1) // slab
    lane_block = iota((na * slab, LANES), 1) // slab

    def gram_of(h):
        stack = jnp.concatenate([rows[h, a] for a in range(na)], axis=1)
        hi, lo = split(stack)
        thi, tlo = split(stack.T)
        total = jnp.zeros((na * slab, LANES), F32)
        for b in range(na):
            at = slice(b * LANES, (b + 1) * LANES)
            wide = dot(thi, hi[:, at]) + dot(thi, lo[:, at]) + dot(tlo, hi[:, at])
            wide = wide.reshape(na, LANES, LANES)
            wide = jnp.where((q_row == q_col)[None], wide, 0.0)
            wide = wide.reshape(na, LANES // slab, slab, LANES).sum(axis=1).reshape(na * slab, LANES)
            shift = LANES // 2
            while shift >= slab:
                wide = wide + pltpu.roll(wide, shift, 1)
                shift //= 2
            total = jnp.where(lane_block == b, wide, total)
        return total

    for h in range(halves):
        project(h)
        for o in an_offsets:
            row_copy(h, o).start()
        rows[h, mine] = proj[h, pl.ds(pl.multiple_of(mine * share, SUB), share), :]

    total = None
    for h in range(halves):
        for o in an_offsets:
            row_copy(h, o).wait()
        gram_half = gram_of(h)
        total = gram_half if total is None else total + gram_half
    part[...] = total.reshape(na, slab, LANES)

    def part_copy(o):
        peer = an_peer(o)
        return pltpu.make_async_remote_copy(
            src_ref=part.at[peer], dst_ref=part_in.at[mine],
            send_sem=part_send.at[o], recv_sem=part_recv.at[o],
            device_id=(me, peer), device_id_type=MESH,
        )

    for o in an_offsets:
        part_copy(o).start()
    part_in[mine] = part[mine]
    for o in an_offsets:
        part_copy(o).wait()
    term[...] = part_in[...].sum(axis=0)

    def term_copy(o):
        return pltpu.make_async_remote_copy(
            src_ref=term, dst_ref=term_in.at[me],
            send_sem=term_send.at[o], recv_sem=term_recv.at[o],
            device_id=(wa_peer(o), mine), device_id_type=MESH,
        )

    for o in wa_offsets:
        term_copy(o).start()
    term_in[me] = term[...]
    for o in wa_offsets:
        term_copy(o).wait()
    out_ref[...] = term_in[...].sum(axis=0)


def on_device(mass_field, factor_one, factor_two, factor_four):
    nw, na = lax.axis_size("wa"), lax.axis_size("an")
    species, fibre, slab, first = mass_field.shape
    rank_one, rank_two, rank_four = factor_one.shape[1], factor_two.shape[1], factor_four.shape[1]
    chunks = 4
    per = fibre // chunks
    halves = rank_one * rank_four * slab // (nw * SUB * LANES)
    kept = rank_two * SUB
    share = kept // na
    depth = nw * per * SUB
    dma = pltpu.SemaphoreType.DMA
    vmem = pl.BlockSpec(memory_space=pltpu.VMEM)
    summed = pl.pallas_call(
        functools.partial(kernel, nw, na, chunks),
        out_shape=jax.ShapeDtypeStruct((slab, LANES), F32),
        in_specs=[pl.BlockSpec(memory_space=pl.ANY)] * 4,
        out_specs=vmem,
        scratch_shapes=[
            pltpu.VMEM((rank_one, first), F32),
            pltpu.VMEM((fibre, rank_two), F32),
            pltpu.VMEM((rank_four, species), F32),
            dma((3,)),
            pltpu.VMEM((fibre, species, slab, first), F32),
            pltpu.VMEM((rank_four * SUB, 3 * species * SUB), BF16),
            pltpu.VMEM((rank_one, 3 * first), BF16),
            pltpu.VMEM((per, rank_four, slab, first), F32),
            pltpu.VMEM((nw, fibre, rank_two), F32),
            pltpu.VMEM((chunks, 2 * kept, depth), BF16),
            pltpu.VMEM((chunks, halves, nw, per, SUB, LANES), F32),
            pltpu.VMEM((chunks, halves, nw, per, SUB, LANES), F32),
            pltpu.VMEM((halves, kept, LANES), F32),
            pltpu.VMEM((halves, na, share, LANES), F32),
            pltpu.VMEM((na, slab, LANES), F32),
            pltpu.VMEM((na, slab, LANES), F32),
            pltpu.VMEM((slab, LANES), F32),
            pltpu.VMEM((nw, slab, LANES), F32),
            dma((fibre,)),
            dma((nw,)), dma((nw,)),
            dma((chunks, halves, nw)), dma((chunks, halves, nw)),
            dma((halves, na)), dma((halves, na)),
            dma((na,)), dma((na,)),
            dma((nw,)), dma((nw,)),
        ],
        compiler_params=pltpu.CompilerParams(
            collective_id=0, has_side_effects=True, vmem_limit_bytes=56 * 1024 * 1024
        ),
    )(mass_field, factor_one.T, factor_two, factor_four.T)
    return summed[:, : na * slab] / (rank_one * rank_two * rank_four)


def solution(mesh):
    in_specs = (P(None, "wa", "an", None), P(), P("wa", None), P())
    out_specs = P("an", None)
    return jax.shard_map(
        on_device, mesh=mesh, in_specs=in_specs, out_specs=out_specs, check_vma=False
    )
```
